32 devices in a mesh: ctx: 16 (over z, y, core), head: 2 (over x).
Axes of the slice: x: 2, y: 2, z: 4, core: 2. Of those that a mesh axis runs over, the one named last changes fastest.
Arguments:
- queries: bfloat16 [8192, 2048], P('ctx', 'head'), may hold values from -120 to 120
- key_vectors: bfloat16 [8192, 128], P('ctx'), may hold values from -7 to 7
- value_vectors: bfloat16 [8192, 128], P('ctx'), may hold values from -6 to 6
- out_grad: bfloat16 [8192, 2048], P('ctx', 'head'), may hold values from -6 to 6
- doc_lengths: int32 [4], replicated, may hold values from 1 to 4096, 8192 in all
- partner_table: int32 [2, 16], replicated, may hold values from 0 to 15, as said below
Outputs:
- query_grad: bfloat16 [8192, 2048], P('ctx', 'head')
- key_grad: float32 [8192, 128], P(('ctx', 'head'))
- value_grad: float32 [8192, 128], P(('ctx', 'head'))
The draws below stay inside these ranges and needn't reach their ends.
Inputs may be any that keep to these rules, and one draw needn't show every extreme that they name: partner_table[t, b] = b XOR m_t for a number m_t of 1 to 15 that is the same for every b; m_0 differs from m_1, so a block's two partners differ from each other and from itself.
All inputs are finite; a program needn't handle non-finite values.
Results may differ from the reference program's by a relative error of at most 0.015.
Values may be sent and summed in bfloat16 or wider, within the bound.
No kernel may reach another device: no remote copies, remote signals or barrier semaphores. Data moves between devices by JAX's collectives and lax.ppermute only.
A program may use at most 128 MiB of HBM per device.

```python
import math
import jax
import jax.numpy as jnp
import numpy as np
from jax import lax

HEADS = 16
HEAD_DIM = 128
STRETCH = 256
ROUNDS = 2
DOCS = 4
TOKENS = 8192
N_CTX = 16


def shared_keys(key):
    return jnp.clip(jax.random.normal(key, (TOKENS, HEAD_DIM), jnp.float32), -6.0, 6.0)


def draw_queries(key, part):
    key = jax.random.fold_in(key, 7)
    return jnp.clip(jax.random.normal(key, (TOKENS, HEADS * HEAD_DIM), jnp.float32), -6.0, 6.0).astype(jnp.bfloat16)


def draw_key_vectors(key, part):
    base_keys = shared_keys(key)
    return base_keys.astype(jnp.bfloat16)


def draw_partner_table(key, part):
    key = jax.random.fold_in(key, 5)
    first_mask = jax.random.randint(key, (1,), 1, N_CTX)
    second_mask = jax.random.randint(jax.random.fold_in(key, 1), (1,), 1, N_CTX - 1)
    second_mask = second_mask + (second_mask >= first_mask).astype(jnp.int32)
    masks = jnp.concatenate([first_mask, second_mask]).astype(jnp.int32)
    return jnp.bitwise_xor(jnp.arange(N_CTX, dtype=jnp.int32)[None, :], masks[:, None]).astype(jnp.int32)


def steps_of(rng, shape, pieces, low, top_value):
    def one(dim, blocks):
        steps = jax.random.uniform(jax.random.fold_in(jax.random.fold_in(rng, 6), dim), (blocks,), jnp.float32, low / len(pieces), top_value / len(pieces))
        return jnp.repeat(jnp.exp(steps), shape[dim] // blocks).reshape((-1,) + (1,) * (len(shape) - dim - 1))

    factor_of = one(*pieces[0])
    for cut in pieces[1:]:
        factor_of = factor_of * one(*cut)
    return factor_of


def length_profile(number_of, total, most, skew):
    portions = [(1 << 20) // math.isqrt(standing ** skew) + 1 for standing in range(2, number_of + 1)]
    surplus, holding = total - most - (number_of - 1), [1] * (number_of - 1)
    while surplus > 0:
        candidates = [i for i in range(number_of - 1) if holding[i] < most]
        whole, remaining = sum([portions[i] for i in candidates]), surplus
        for i in candidates:
            more = min(most - holding[i], max(1, remaining * portions[i] // whole), surplus)
            holding[i] = holding[i] + more
            surplus = surplus - more
    return np.array([most] + holding)


def uneven_parts(rng, count, total, reach, lean):
    if count == 2:
        one = jax.random.randint(rng, (), max(1, total - reach), min(reach, total - 1) + 1)
        return jnp.stack([one, total - one])
    tallies = jnp.asarray(length_profile(count, total, reach, lean), jnp.int32)
    pairs = (count - 1) // 2
    source_of, taker = tallies[1:1 + 2 * pairs:2], tallies[2:2 + 2 * pairs:2]
    margin = jnp.minimum(source_of - 1, reach - taker)
    passed = jax.random.randint(jax.random.fold_in(rng, 1), (pairs,), 0, 1 << 20) % (margin + 1)
    tallies = tallies.at[1:1 + 2 * pairs:2].set(source_of - passed).at[2:2 + 2 * pairs:2].set(taker + passed)
    return tallies[jax.random.permutation(jax.random.fold_in(rng, 2), count)]


def normal_values(own_key, dims, width, reach, pieces=(), kind=jnp.bfloat16):
    gain = steps_of(own_key, dims, pieces, -0.22, 0.18) if pieces else 1.0
    entries = jax.random.normal(own_key, dims, jnp.float32) * width * gain
    return jnp.minimum(jnp.maximum(entries, -reach), reach).astype(kind)


def setup_inputs(seed: int = 0) -> dict:
    streams_of = jax.random.split(jax.random.key(seed), 7)
    queries = draw_queries(jax.random.fold_in(streams_of[6], 71), 0)
    key_vectors = draw_key_vectors(jax.random.fold_in(streams_of[6], 71), 0)
    value_vectors = normal_values(streams_of[2], (TOKENS, HEAD_DIM), 1.0, 6.0, ((0, 16),))
    out_grad = normal_values(streams_of[3], (TOKENS, HEADS * HEAD_DIM), 1.0, 6.0, ((0, 16), (1, 2)))
    doc_lengths = uneven_parts(streams_of[4], DOCS, TOKENS, TOKENS // 2, 2).astype(jnp.int32)
    partner_table = draw_partner_table(jax.random.fold_in(streams_of[6], 71), 0)
    return {"queries": queries, "key_vectors": key_vectors, "value_vectors": value_vectors, "out_grad": out_grad, "doc_lengths": doc_lengths, "partner_table": partner_table}


def stored_positions(block_index, stretch_len, blocks):
    local_rows = jnp.arange(2 * stretch_len, dtype=jnp.int32)
    stretch_index = jnp.where(local_rows < stretch_len, block_index, 2 * blocks - 1 - block_index)
    return (stretch_index * stretch_len + local_rows % stretch_len).astype(jnp.int32)


def documents(positions, doc_ends):
    return jnp.sum((positions[:, None] >= doc_ends[None, :]).astype(jnp.int32), axis=1)


def head_grads(query_rows, cotangent, key_all, value_all, visible):
    factor = query_rows.shape[1] ** -0.5
    scores = jnp.dot(query_rows, key_all.T, preferred_element_type=jnp.float32) * factor
    masked = jnp.where(visible, scores, -jnp.inf)
    largest = jnp.max(masked, axis=1, keepdims=True)
    weights = jnp.exp(masked - largest)
    prob_full = weights / jnp.sum(weights, axis=1, keepdims=True)
    prob_low = prob_full.astype(jnp.bfloat16)
    attended = jnp.dot(prob_low, value_all, preferred_element_type=jnp.float32)
    row_delta = jnp.sum(cotangent.astype(jnp.float32) * attended, axis=1, keepdims=True)
    dprobs = jnp.dot(cotangent, value_all.T, preferred_element_type=jnp.float32)
    dscores = (prob_full * (dprobs - row_delta)).astype(jnp.bfloat16)
    query_part = jnp.dot(dscores, key_all, preferred_element_type=jnp.float32) * factor
    key_part = jnp.dot(dscores.T, query_rows, preferred_element_type=jnp.float32) * factor
    value_part = jnp.dot(prob_low.T, cotangent, preferred_element_type=jnp.float32)
    return query_part, key_part, value_part


def reference(queries, key_vectors, value_vectors, out_grad, doc_lengths, partner_table):
    block_rows = 2 * STRETCH
    doc_ends = jnp.cumsum(doc_lengths)[:-1].astype(jnp.int32)

    def one_block(running, block_index):
        key_grad, value_grad = running
        owners = jnp.concatenate([block_index[None], partner_table[:, block_index]]).astype(jnp.int32)
        starts = (owners * block_rows).astype(jnp.int32)
        key_all = jnp.concatenate([lax.dynamic_slice_in_dim(key_vectors, starts[owner_slot], block_rows, 0) for owner_slot in range(ROUNDS + 1)], axis=0)
        value_all = jnp.concatenate([lax.dynamic_slice_in_dim(value_vectors, starts[owner_slot], block_rows, 0) for owner_slot in range(ROUNDS + 1)], axis=0)
        key_pos = jnp.concatenate([stored_positions(owners[owner_slot], STRETCH, N_CTX) for owner_slot in range(ROUNDS + 1)])
        query_pos = stored_positions(block_index, STRETCH, N_CTX)
        same_doc = documents(key_pos, doc_ends)[None, :] == documents(query_pos, doc_ends)[:, None]
        visible = (key_pos[None, :] <= query_pos[:, None]) & same_doc
        start_row = (block_index * block_rows).astype(jnp.int32)
        query_block = lax.dynamic_slice_in_dim(queries, start_row, block_rows, 0)
        grad_block = lax.dynamic_slice_in_dim(out_grad, start_row, block_rows, 0)
        query_parts = []
        key_total = jnp.zeros(((ROUNDS + 1) * block_rows, HEAD_DIM), jnp.float32)
        value_total = jnp.zeros(((ROUNDS + 1) * block_rows, HEAD_DIM), jnp.float32)
        for column in range(HEADS):
            head_query = query_block[:, column * HEAD_DIM:(column + 1) * HEAD_DIM]
            head_grad = grad_block[:, column * HEAD_DIM:(column + 1) * HEAD_DIM]
            query_part, key_part, value_part = head_grads(head_query, head_grad, key_all, value_all, visible)
            query_parts.append(query_part)
            key_total = key_total + key_part
            value_total = value_total + value_part
        for owner_slot in range(ROUNDS + 1):
            lower = owner_slot * block_rows
            upper = lower + block_rows
            key_grad = lax.dynamic_update_slice_in_dim(key_grad, lax.dynamic_slice_in_dim(key_grad, starts[owner_slot], block_rows, 0) + key_total[lower:upper], starts[owner_slot], 0)
            value_grad = lax.dynamic_update_slice_in_dim(value_grad, lax.dynamic_slice_in_dim(value_grad, starts[owner_slot], block_rows, 0) + value_total[lower:upper], starts[owner_slot], 0)
        return (key_grad, value_grad), jnp.concatenate(query_parts, axis=1).astype(jnp.bfloat16)

    empty_grad = jnp.zeros((TOKENS, HEAD_DIM), jnp.float32)
    (key_grad, value_grad), query_grad = lax.scan(one_block, (empty_grad, empty_grad), jnp.arange(N_CTX, dtype=jnp.int32))
    return query_grad.reshape(TOKENS, HEADS * HEAD_DIM), key_grad, value_grad
```

```python
from functools import partial

import jax
import jax.numpy as jnp
from jax import lax
from jax.experimental import pallas as pl
from jax.experimental.pallas import tpu as pltpu
from jax.sharding import PartitionSpec as P

LOG2E = 1.4426950408889634
MASKED = -1e30
BF16 = jnp.bfloat16
F32 = jnp.float32
SMALL = 6 * 2**20
VMEM_LIMITS = (14 * 2**20, 12 * 2**20)


def nt_dot(left, right):
    return lax.dot_general(left, right, (((1,), (1,)), ((), ())), preferred_element_type=F32)


def nn_dot(left, right):
    return lax.dot_general(left, right, (((1,), (0,)), ((), ())), preferred_element_type=F32)


def document_start(ends, position):
    start = jnp.zeros_like(position)
    for end in ends:
        start = jnp.maximum(start, jnp.where(position >= end, end, 0))
    return start


def sees(ends, piece, query_piece, key_piece):
    return (key_piece <= query_piece) & (
        key_piece * piece + piece - 1 >= document_start(ends, query_piece * piece)
    )


def chip_pairs(blocks):
    return [(small, large) for large in range(1, blocks // 2) for small in range(large + 1)]


def plan_kernel(
    blocks,
    doc_hbm,
    table_hbm,
    k_hbm,
    v_hbm,
    plan_ref,
    flip0_ref,
    flip1_ref,
    index_ref,
    fetch_ref,
    middle_ref,
    k_ref,
    v_ref,
    rows_ref,
    doc_ref,
    table_ref,
    sem,
):
    pairs = ((doc_hbm, doc_ref), (table_hbm, table_ref), (k_hbm, k_ref), (v_hbm, v_ref))
    copies = [pltpu.make_async_copy(*pair, sem.at[number]) for number, pair in enumerate(pairs)]
    for copy in copies:
        copy.start()
    piece = k_ref.shape[0] // 2
    block = lax.axis_index("ctx")
    side = lax.axis_index("head")
    for copy in copies[:2]:
        copy.wait()
    ends = []
    running = 0
    for doc in range(doc_ref.shape[0] - 1):
        running = running + doc_ref[doc]
        ends.append(running)
    first, second = table_ref[0, 0], table_ref[1, 0]
    flips = jnp.minimum(first, second), jnp.maximum(first, second)

    half_way = blocks * piece
    start, stop = jnp.int32(0), jnp.int32(2 * half_way)
    for end in reversed(ends):
        start = jnp.where(end <= half_way, jnp.maximum(start, end), start)
        stop = jnp.where(end > half_way, end, stop)
    first_key = lax.div(start, piece)
    first_query = 2 * blocks - 1 - lax.div(stop - 1, piece)
    middle = jnp.int32(0)
    for other in range(blocks):
        for flip in flips:
            middle = middle | ((other >= first_query) & ((other ^ flip) >= first_key)).astype(jnp.int32)

    for place, number in enumerate((*ends, *flips, middle)):
        plan_ref[place] = number
    small, large = (lax.shift_right_logical(flip, 1) for flip in flips)
    flip0_ref[0] = small
    flip1_ref[0] = large
    pair = lax.shift_right_logical(large * (large + 1), 1) + small - 1
    index_ref[0] = pair
    fetch_ref[0] = pair + middle * len(chip_pairs(blocks))
    middle_ref[0] = middle
    for number, flip in enumerate(flips):
        odd = flip & 1
        source = block ^ odd
        upper = (source > (source ^ flip)).astype(jnp.int32) * (1 - middle * side)
        for place, value in ((2 * number, odd), (2 * number + 1, upper)):
            rows_ref[place : place + 1, :] = jnp.full((1, rows_ref.shape[1]), value.astype(F32))
    for copy in copies[2:]:
        copy.wait()


def make_plan(blocks, doc_lengths, table, keys, values):
    smem = pl.BlockSpec(memory_space=pltpu.SMEM)
    vmem = pl.BlockSpec(memory_space=pltpu.VMEM)
    hbm = pl.BlockSpec(memory_space=pltpu.HBM)
    scalar = jax.ShapeDtypeStruct((1,), jnp.int32)
    pair = jax.ShapeDtypeStruct(keys.shape, keys.dtype)
    return pl.pallas_call(
        lambda *refs: plan_kernel(blocks, *refs),
        out_shape=[jax.ShapeDtypeStruct((8,), jnp.int32)]
        + [scalar] * 5
        + [pair, pair, jax.ShapeDtypeStruct((8, keys.shape[1]), F32)],
        in_specs=[hbm] * 4,
        out_specs=[smem] * 6 + [vmem] * 3,
        scratch_shapes=[
            pltpu.SMEM(doc_lengths.shape, jnp.int32),
            pltpu.SMEM(table.shape, jnp.int32),
            pltpu.SemaphoreType.DMA((4,)),
        ],
        compiler_params=pltpu.CompilerParams(vmem_limit_bytes=SMALL),
        cost_estimate=pl.CostEstimate(flops=0, bytes_accessed=4 * keys.size, transcendentals=0),
        name="plan",
    )(*[pltpu.with_memory_space_constraint(part, pltpu.HBM) for part in (doc_lengths, table, keys, values)])


def message_kernel(rows_ref, k_ref, v_ref, k2_ref, v2_ref, *message_refs):
    piece = k_ref.shape[0] // 2
    halves = slice(0, piece), slice(piece, 2 * piece)
    for number, message_ref in enumerate(message_refs):
        odd = rows_ref[2 * number : 2 * number + 1, :] > 0.5
        upper = rows_ref[2 * number + 1 : 2 * number + 2, :] > 0.5
        for target, own_ref, sibling_ref in ((halves[0], k_ref, k2_ref), (halves[1], v_ref, v2_ref)):
            low, high = (
                jnp.where(odd, sibling_ref[half].astype(F32), own_ref[half].astype(F32)) for half in halves
            )
            message_ref[target] = jnp.where(upper, high, low).astype(message_ref.dtype)


def make_messages(rows, *pairs):
    vmem = pl.BlockSpec(memory_space=pltpu.VMEM)
    message = jax.ShapeDtypeStruct(pairs[0].shape, pairs[0].dtype)
    return pl.pallas_call(
        message_kernel,
        out_shape=[message] * 2,
        in_specs=[vmem] * 5,
        out_specs=[vmem] * 2,
        compiler_params=pltpu.CompilerParams(vmem_limit_bytes=SMALL),
        name="messages",
    )(rows, *pairs)


def sum_pairs_kernel(keep_ref, received_ref, *out_refs):
    rows = out_refs[0].shape[0]
    for place, out_ref in enumerate(out_refs):
        part = slice(place * rows, (place + 1) * rows)
        out_ref[...] = (keep_ref[part] + received_ref[part].astype(F32)).astype(out_ref.dtype)


def sum_own_kernel(rows_ref, own_ref, own_received_ref, *refs):
    *back_refs, total_ref = refs
    total = own_ref[...] + own_received_ref[...].astype(F32)
    for number, back_ref in enumerate(back_refs):
        odd = rows_ref[2 * number : 2 * number + 1, :] > 0.5
        total = total + jnp.where(odd, 0.0, back_ref[...].astype(F32))
    total_ref[...] = total


def sum_all_kernel(rows_ref, total_ref, *refs):
    *sibling_refs, key_ref, value_ref = refs
    piece = key_ref.shape[0]
    for out_ref, rows in ((key_ref, slice(0, piece)), (value_ref, slice(piece, 2 * piece))):
        total = total_ref[rows]
        for number, sibling_ref in enumerate(sibling_refs):
            odd = rows_ref[2 * number : 2 * number + 1, :] > 0.5
            total = total + jnp.where(odd, sibling_ref[rows].astype(F32), 0.0)
        out_ref[...] = total


def head_copies(heads, width, hbm_ref, vmem_ref, sem, out=False):
    copies = []
    for head in range(heads):
        columns = hbm_ref.at[:, head * width : (head + 1) * width]
        ends = (vmem_ref.at[head], columns) if out else (columns, vmem_ref.at[head])
        copies.append(pltpu.make_async_copy(*ends, sem.at[head]))
    return copies


def piece_rows(slot, piece):
    return pl.ds(pl.multiple_of(slot * piece, piece), piece)


def partner_tiles(ends, flips, blocks, piece, block, tiles, first):
    count = jnp.int32(first)
    for round_index, flip in enumerate(flips):
        other = block ^ flip
        for query_slot, query_piece, key_slot, key_piece in (
            (0, block, 2 * round_index + 2, other),
            (1, 2 * blocks - 1 - block, 2 * round_index + 2, other),
            (1, 2 * blocks - 1 - block, 2 * round_index + 3, 2 * blocks - 1 - other),
        ):
            active = sees(ends, piece, query_piece, key_piece)

            @pl.when(active)
            def _():
                tiles[0, count] = jnp.int32(query_slot)
                tiles[1, count] = jnp.int32(key_slot)
                tiles[2, count] = query_piece * piece
                tiles[3, count] = key_piece * piece

            count = count + active.astype(jnp.int32)
    return count


def tile_gradients(heads, piece, e_ref, dp_ref, scale_ref, delta_ref, q_ref, g_ref, dk_acc, dv_acc, together=4):
    width = q_ref.shape[2]

    def run(index, query_slot, key_slot, hand_on):
        query_rows = piece_rows(query_slot, piece)
        key_rows = piece_rows(key_slot, piece)

        def elementwise(group):
            lows, ds = [], []
            for head in range(group * together, (group + 1) * together):
                row = slice(head, head + 1)
                probs = e_ref[index, head] * scale_ref[index, row, :]
                lows.append(probs.astype(BF16))
                ds.append((probs * (dp_ref[index, head] - delta_ref[query_slot, row, :])).astype(BF16))
            return jnp.concatenate(lows, axis=1), jnp.concatenate(ds, axis=1)

        def products(group, probs, dscores, dk, dv):
            members = slice(group * together, (group + 1) * together)
            dv = dv + nn_dot(probs, g_ref[members, query_rows, :].reshape(together * piece, width))
            dk = dk + nn_dot(dscores, q_ref[members, query_rows, :].reshape(together * piece, width))
            hand_on(slice(group * together * piece, (group + 1) * together * piece), dscores)
            return dk, dv

        dk = jnp.zeros((piece, width), F32)
        dv = jnp.zeros((piece, width), F32)
        held = elementwise(0)
        for group in range(1, heads // together):
            following = elementwise(group)
            dk, dv = products(group - 1, *held, dk, dv)
            held = following
        dk, dv = products(heads // together - 1, *held, dk, dv)
        dk_acc[key_rows, :] += dk
        dv_acc[key_rows, :] += dv

    return run


def partner_kernel(
    blocks,
    heads,
    plan_hbm,
    q_hbm,
    g_hbm,
    k_ref,
    v_ref,
    first0_hbm,
    second0_hbm,
    first1_hbm,
    second1_hbm,
    keep_ref,
    cross_ref,
    e_buf,
    dp_buf,
    ds_all,
    stat_l,
    delta_buf,
    q_ref,
    g_ref,
    kall,
    plan_ref,
    plan_sem,
    head_sem,
    pair_sem,
    vall,
    bias_buf,
    stat_m,
    stat_d,
    dk_acc,
    dv_acc,
    tiles,
):
    rows, width = k_ref.shape
    piece = rows // 2
    factor = width**-0.5
    block = lax.axis_index("ctx")
    side = lax.axis_index("head")
    rounds = 2
    own_tiles = 3
    slots = stat_m.shape[0]

    plan_copy = pltpu.make_async_copy(plan_hbm, plan_ref, plan_sem.at[0])
    plan_copy.start()
    arrivals_by_head = list(
        zip(
            head_copies(heads, width, q_hbm, q_ref, head_sem.at[0]),
            head_copies(heads, width, g_hbm, g_ref, head_sem.at[1]),
        )
    )
    for arrivals in arrivals_by_head:
        for arrival in arrivals:
            arrival.start()
    kall[:rows] = k_ref[...]
    vall[:rows] = v_ref[...]
    stat_m[...] = jnp.full_like(stat_m, 2 * MASKED)
    stat_l[...] = jnp.zeros_like(stat_l)
    stat_d[...] = jnp.zeros_like(stat_d)
    plan_copy.wait()
    docs = 3
    ends = [plan_ref[doc] for doc in range(docs)]
    flips = [plan_ref[docs], plan_ref[docs + 1]]
    middle = plan_ref[docs + 2]
    pairs = []
    for round_index, received in enumerate(((first0_hbm, second0_hbm), (first1_hbm, second1_hbm))):
        half = (block < (block ^ flips[round_index])).astype(jnp.int32) * (1 - middle * side)
        for both, where in zip(received, (half, 1 - half)):
            place = pl.ds(pl.multiple_of((2 * round_index + 2 + where) * piece, piece), piece)
            pairs += [(both.at[:piece], kall.at[place]), (both.at[piece:], vall.at[place])]
    pair_arrivals = [pltpu.make_async_copy(*pair, pair_sem.at[number]) for number, pair in enumerate(pairs)]
    for arrival in pair_arrivals:
        arrival.start()

    low_piece = block
    high_piece = 2 * blocks - 1 - block
    own = [(0, 0, low_piece, low_piece), (1, 1, high_piece, high_piece), (1, 0, high_piece, low_piece)]
    for index, (query_slot, key_slot, query_piece, key_piece) in enumerate(own):
        tiles[0, index] = jnp.int32(query_slot)
        tiles[1, index] = jnp.int32(key_slot)
        tiles[2, index] = query_piece * piece
        tiles[3, index] = key_piece * piece
    own_active = sees(ends, piece, high_piece, low_piece)
    count = partner_tiles(ends, flips, blocks, piece, block, tiles, own_tiles)

    def set_bias(index, slot):
        query_start = tiles[2, index]
        key_start = tiles[3, index]
        query_pos = query_start + lax.broadcasted_iota(jnp.int32, (1, piece), 1)
        starts = document_start(ends, query_pos)
        key_index = lax.broadcasted_iota(jnp.int32, (piece, piece), 0)
        seen = (key_index >= starts - key_start) & (key_index <= query_pos - key_start)
        bias_buf[slot] = jnp.where(seen, 0.0, MASKED)

    def head_scores(index, head, query_slot, query_rows, keys, values, slot, from_diagonal):
        row = slice(head, head + 1)
        scores = nt_dot(keys, q_ref[head, query_rows, :]) * (factor * LOG2E) + bias_buf[slot]
        if from_diagonal:
            top = stat_m[query_slot, row, :]
        else:
            top = jnp.max(scores, axis=0, keepdims=True)
        weights = jnp.exp2(scores - top)
        dprobs = nt_dot(values, g_ref[head, query_rows, :])
        e_buf[index, head] = weights
        dp_buf[index, head] = dprobs
        stat_m[index, row, :] = top
        stat_l[index, row, :] = jnp.sum(weights, axis=0, keepdims=True)
        stat_d[index, row, :] = jnp.sum(weights * dprobs, axis=0, keepdims=True)

    def first_pass(from_diagonal):
        def run(index, carry):
            query_slot = tiles[0, index]
            query_rows = piece_rows(query_slot, piece)
            key_rows = piece_rows(tiles[1, index], piece)
            set_bias(index, 0)
            keys = kall[key_rows, :]
            values = vall[key_rows, :]
            for head in range(heads):
                head_scores(index, head, query_slot, query_rows, keys, values, 0, from_diagonal)
            return carry

        return run

    for index in range(2):
        set_bias(index, index)
    for head, arrivals in enumerate(arrivals_by_head):
        for arrival in arrivals:
            arrival.wait()
        for index in range(2):
            part = slice(index * piece, (index + 1) * piece)
            head_scores(index, head, index, part, kall[part, :], vall[part, :], index, False)
    dk_acc[...] = jnp.zeros_like(dk_acc)
    dv_acc[...] = jnp.zeros_like(dv_acc)
    for arrival in pair_arrivals:
        arrival.wait()
    begin = jnp.where(own_active, own_tiles - 1, own_tiles)
    lax.fori_loop(begin, count, first_pass(True), 0)
    redo = jnp.max(stat_l[...]) > 2.0**80
    lax.fori_loop(begin, jnp.where(redo, count, begin), first_pass(False), 0)

    lower = [tiles[0, slot] == 0 for slot in range(slots)]
    nothing = jnp.full((heads, piece), 2 * MASKED, F32)
    tops = [nothing, nothing]
    for slot in range(slots):
        top = stat_m[slot]
        tops[0] = jnp.maximum(tops[0], jnp.where(lower[slot], top, nothing))
        tops[1] = jnp.maximum(tops[1], jnp.where(lower[slot], nothing, top))
    scales = [jnp.exp2(stat_m[slot] - jnp.where(lower[slot], *tops)) for slot in range(slots)]
    zero = jnp.zeros((heads, piece), F32)
    totals, deltas = [zero, zero], [zero, zero]
    for slot in range(slots):
        part, share = scales[slot] * stat_l[slot], scales[slot] * stat_d[slot]
        totals = [totals[0] + jnp.where(lower[slot], part, zero), totals[1] + jnp.where(lower[slot], zero, part)]
        deltas = [deltas[0] + jnp.where(lower[slot], share, zero), deltas[1] + jnp.where(lower[slot], zero, share)]
    inverses = [1.0 / total for total in totals]
    for query_slot in range(2):
        delta_buf[query_slot] = deltas[query_slot] * inverses[query_slot]
    for slot in range(slots):
        stat_l[slot] = scales[slot] * jnp.where(lower[slot], *inverses)

    add_tile = tile_gradients(heads, piece, e_buf, dp_buf, stat_l, delta_buf, q_ref, g_ref, dk_acc, dv_acc)

    def second_pass(index, carry):
        def keep_dscores(columns, dscores):
            ds_all[index - own_tiles, :, columns] = dscores

        add_tile(index, tiles[0, index], tiles[1, index], keep_dscores)
        return carry

    lax.fori_loop(own_tiles, count, second_pass, 0)

    for place in range(rounds):
        base = place * rows
        for half, out_ref in ((side, keep_ref), (1 - side, cross_ref)):
            key_rows = pl.ds(pl.multiple_of((2 * place + 2 + half) * piece, piece), piece)
            out_ref[base : base + piece] = (dk_acc[key_rows, :] * factor).astype(out_ref.dtype)
            out_ref[base + piece : base + rows] = dv_acc[key_rows, :].astype(out_ref.dtype)


def own_kernel(
    blocks,
    heads,
    plan_ref,
    e_ref,
    dp_ref,
    ds_all,
    scale_ref,
    delta_ref,
    q_ref,
    g_ref,
    kall,
    dq_hbm,
    own_ref,
    own_cross_ref,
    dq_ref,
    out_sem,
    dk_acc,
    dv_acc,
    dqt_acc,
    tiles,
):
    _, rows, width = q_ref.shape
    piece = rows // 2
    factor = width**-0.5
    block = lax.axis_index("ctx")
    side = lax.axis_index("head")
    docs = 3
    own_tiles = 3
    ends = [plan_ref[doc] for doc in range(docs)]
    flips = [plan_ref[docs], plan_ref[docs + 1]]
    dk_acc[...] = jnp.zeros_like(dk_acc)
    dv_acc[...] = jnp.zeros_like(dv_acc)
    dqt_acc[...] = jnp.zeros_like(dqt_acc)
    add_tile = tile_gradients(heads, piece, e_ref, dp_ref, scale_ref, delta_ref, q_ref, g_ref, dk_acc, dv_acc)

    def own_tile(index, carry):
        query_slot, key_slot = jnp.minimum(index, 1), index & 1
        keys_t = kall[piece_rows(key_slot, piece), :].T

        def add_query_gradient(columns, dscores):
            dqt_acc[query_slot, :, columns] += nn_dot(keys_t, dscores)

        add_tile(index, query_slot, key_slot, add_query_gradient)
        return carry

    own_active = sees(ends, piece, 2 * blocks - 1 - block, block)
    lax.fori_loop(0, jnp.where(own_active, own_tiles, own_tiles - 1), own_tile, 0)

    def partner_tile(index, carry):
        keys_t = kall[piece_rows(tiles[1, index], piece), :].T
        dqt_acc[tiles[0, index]] += nn_dot(keys_t, ds_all[index])
        return carry

    lax.fori_loop(0, partner_tiles(ends, flips, blocks, piece, block, tiles, 0), partner_tile, 0)

    leaving = head_copies(heads, width, dq_hbm, dq_ref, out_sem, out=True)
    for head in range(heads):
        for query_slot in range(2):
            dq_ref[head, query_slot * piece : (query_slot + 1) * piece, :] = (
                (dqt_acc[query_slot, :, head * piece : (head + 1) * piece] * factor).astype(BF16).T
            )
        leaving[head].start()
    for half, out_ref in ((side, own_ref), (1 - side, own_cross_ref)):
        key_rows = pl.ds(pl.multiple_of(half * piece, piece), piece)
        out_ref[:piece] = (dk_acc[key_rows, :] * factor).astype(out_ref.dtype)
        out_ref[piece:] = dv_acc[key_rows, :].astype(out_ref.dtype)
    for copy in leaving:
        copy.wait()


def partner_attention(blocks, plan, queries, out_grad, keys, values, remote):
    rows, width = keys.shape
    heads = queries.shape[1] // width
    piece = rows // 2
    most = 7
    vmem = pl.BlockSpec(memory_space=pltpu.VMEM)
    hbm = pl.BlockSpec(memory_space=pltpu.HBM)
    anywhere = pl.BlockSpec(memory_space=pl.ANY)
    return pl.pallas_call(
        lambda *refs: partner_kernel(blocks, heads, *refs),
        out_shape=[
            jax.ShapeDtypeStruct((2 * rows, width), F32),
            jax.ShapeDtypeStruct((2 * rows, width), BF16),
            jax.ShapeDtypeStruct((most, heads, piece, piece), F32),
            jax.ShapeDtypeStruct((most, heads, piece, piece), F32),
            jax.ShapeDtypeStruct((most - 3, piece, heads * piece), BF16),
            jax.ShapeDtypeStruct((most, heads, piece), F32),
            jax.ShapeDtypeStruct((2, heads, piece), F32),
            jax.ShapeDtypeStruct((heads, rows, width), BF16),
            jax.ShapeDtypeStruct((heads, rows, width), BF16),
            jax.ShapeDtypeStruct((3 * rows, width), BF16),
        ],
        in_specs=[anywhere] + [hbm] * 2 + [vmem] * 2 + [anywhere] * 4,
        out_specs=[vmem] * 10,
        scratch_shapes=[
            pltpu.SMEM(plan.shape, jnp.int32),
            pltpu.SemaphoreType.DMA((1,)),
            pltpu.SemaphoreType.DMA((2, heads)),
            pltpu.SemaphoreType.DMA((8,)),
            pltpu.VMEM((3 * rows, width), BF16),
            pltpu.VMEM((2, piece, piece), F32),
            pltpu.VMEM((most, heads, piece), F32),
            pltpu.VMEM((most, heads, piece), F32),
            pltpu.VMEM((3 * rows, width), F32),
            pltpu.VMEM((3 * rows, width), F32),
            pltpu.SMEM((4, most), jnp.int32),
        ],
        compiler_params=pltpu.CompilerParams(vmem_limit_bytes=VMEM_LIMITS[0]),
        cost_estimate=pl.CostEstimate(
            flops=7 * heads * 4 * 2 * piece * piece * width,
            bytes_accessed=4 * queries.size,
            transcendentals=7 * heads * piece * piece,
        ),
        name="partner_gradients",
    )(
        plan,
        *[pltpu.with_memory_space_constraint(part, pltpu.HBM) for part in (queries, out_grad)],
        keys,
        values,
        *remote,
    )


def own_attention(blocks, plan, *held):
    heads, rows, width = held[-2].shape
    piece = rows // 2
    vmem = pl.BlockSpec(memory_space=pltpu.VMEM)
    smem = pl.BlockSpec(memory_space=pltpu.SMEM)
    hbm = pl.BlockSpec(memory_space=pltpu.HBM)
    return pl.pallas_call(
        lambda *refs: own_kernel(blocks, heads, *refs),
        out_shape=[
            jax.ShapeDtypeStruct((rows, heads * width), BF16),
            jax.ShapeDtypeStruct((rows, width), F32),
            jax.ShapeDtypeStruct((rows, width), BF16),
        ],
        in_specs=[smem] + [vmem] * 8,
        out_specs=[hbm, vmem, vmem],
        scratch_shapes=[
            pltpu.VMEM((heads, rows, width), BF16),
            pltpu.SemaphoreType.DMA((heads,)),
            pltpu.VMEM((rows, width), F32),
            pltpu.VMEM((rows, width), F32),
            pltpu.VMEM((2, width, heads * piece), F32),
            pltpu.SMEM((4, 4), jnp.int32),
        ],
        compiler_params=pltpu.CompilerParams(vmem_limit_bytes=VMEM_LIMITS[1]),
        cost_estimate=pl.CostEstimate(
            flops=3 * heads * 3 * 2 * piece * piece * width,
            bytes_accessed=6 * heads * rows * width,
            transcendentals=0,
        ),
        name="own_gradients",
    )(plan, *held)


def unwritten(like):
    return pl.pallas_call(
        lambda *refs: None,
        out_shape=[jax.ShapeDtypeStruct(like.shape, like.dtype)] * 2,
        out_specs=[pl.BlockSpec(memory_space=pl.ANY)] * 2,
        compiler_params=pltpu.CompilerParams(vmem_limit_bytes=SMALL),
        name="unwritten",
    )()


def swap(message):
    return lax.ppermute(message, "head", [(0, 1), (1, 0)])


def move(blocks, flip, message):
    return lax.ppermute(message, "ctx", [(block, block ^ 2 * flip) for block in range(blocks)]) if flip else message


def few_pairs(blocks):
    return len(chip_pairs(blocks)) <= 64


def one_by_one(blocks, flips, messages):
    branches = [partial(move, blocks, flip) for flip in range(blocks // 2)]
    return [lax.switch(flip.reshape(()), branches, message) for flip, message in zip(flips, messages)]


def fetch(blocks, index, flips, middle, messages):
    def without(pair, *messages):
        return (*[move(blocks, flip, message) for flip, message in zip(pair, messages)], *unwritten(messages[0]))

    def with_middle(pair, *messages):
        moved = [move(blocks, flip, message) for flip, message in zip(pair, messages)]
        return (*moved, *[swap(message) for message in moved])

    if few_pairs(blocks):
        branches = [partial(run, pair) for run in (without, with_middle) for pair in chip_pairs(blocks)]
        return lax.switch(index.reshape(()), branches, *messages)
    moved = one_by_one(blocks, flips, messages)
    swaps = [lambda a, b: tuple(unwritten(a)), lambda a, b: (swap(a), swap(b))]
    return (*moved, *lax.switch(middle.reshape(()), swaps, *moved))


def give_back(blocks, index, flips, messages, aside):
    def run(pair, first, second, aside):
        return move(blocks, pair[0], first), move(blocks, pair[1], second), swap(aside)

    if few_pairs(blocks):
        return lax.switch(index.reshape(()), [partial(run, pair) for pair in chip_pairs(blocks)], *messages, aside)
    return (*one_by_one(blocks, flips, messages), swap(aside))


def on_device(queries, key_vectors, value_vectors, out_grad, doc_lengths, partner_table):
    blocks = lax.axis_size("ctx")
    rows, width = key_vectors.shape

    def sibling(message):
        return lax.ppermute(message, "ctx", [(block, block ^ 1) for block in range(blocks)])

    plan, flip0, flip1, index, fetch_index, middle, keys, values, selectors = make_plan(
        blocks, doc_lengths, partner_table, key_vectors, value_vectors
    )
    messages = make_messages(selectors, keys, values, sibling(key_vectors), sibling(value_vectors))
    first0, first1, second0, second1 = fetch(blocks, fetch_index, (flip0, flip1), middle, messages)
    keep, cross, *held = partner_attention(
        blocks, plan, queries, out_grad, keys, values, (first0, second0, first1, second1)
    )
    received = swap(cross)
    query_grad, own, own_cross = own_attention(blocks, plan, *held)
    vmem = pl.BlockSpec(memory_space=pltpu.VMEM)
    message = jax.ShapeDtypeStruct((rows, width), BF16)
    sums = pl.pallas_call(
        sum_pairs_kernel,
        out_shape=[message] * 2,
        in_specs=[vmem] * 2,
        out_specs=[vmem] * 2,
        compiler_params=pltpu.CompilerParams(vmem_limit_bytes=SMALL),
        name="sum_over_heads",
    )(keep, received)
    *back, own_received = give_back(blocks, index, (flip0, flip1), sums, own_cross)
    traded = [sibling(part) for part in back]
    total = pl.pallas_call(
        sum_own_kernel,
        out_shape=jax.ShapeDtypeStruct((rows, width), F32),
        in_specs=[vmem] * 5,
        out_specs=vmem,
        compiler_params=pltpu.CompilerParams(vmem_limit_bytes=SMALL),
        cost_estimate=pl.CostEstimate(flops=4 * rows * width, bytes_accessed=14 * rows * width, transcendentals=0),
        name="sum_own",
    )(selectors, own, own_received, *back)
    grad = jax.ShapeDtypeStruct((rows // 2, width), F32)
    key_grad, value_grad = pl.pallas_call(
        sum_all_kernel,
        out_shape=[grad] * 2,
        in_specs=[vmem] * 4,
        out_specs=[vmem] * 2,
        compiler_params=pltpu.CompilerParams(vmem_limit_bytes=SMALL),
        name="sum_over_blocks",
    )(selectors, total, *traded)
    return query_grad, key_grad, value_grad


def solution(mesh):
    return jax.shard_map(
        on_device,
        mesh=mesh,
        in_specs=(P("ctx", "head"), P("ctx", None), P("ctx", None), P("ctx", "head"), P(), P()),
        out_specs=(P("ctx", "head"), P(("ctx", "head"), None), P(("ctx", "head"), None)),
        check_vma=False,
    )
```

```python
from functools import partial

import jax
import jax.numpy as jnp
from jax import lax
from jax.experimental import pallas as pl
from jax.experimental.pallas import tpu as pltpu
from jax.sharding import PartitionSpec as P

LOG2E = 1.4426950408889634
MASKED = -1e30
BF16 = jnp.bfloat16
F32 = jnp.float32
SMALL = 4 * 2**20
AHEAD = 3
VMEM_LIMITS = (9 * 2**20, 8 * 2**20)


def nt_dot(left, right):
    return lax.dot_general(left, right, (((1,), (1,)), ((), ())), preferred_element_type=F32)


def nn_dot(left, right):
    return lax.dot_general(left, right, (((1,), (0,)), ((), ())), preferred_element_type=F32)


def document_start(ends, position):
    start = jnp.zeros_like(position)
    for end in ends:
        start = jnp.maximum(start, jnp.where(position >= end, end, 0))
    return start


def sees(ends, piece, query_piece, key_piece):
    return (key_piece <= query_piece) & (
        key_piece * piece + piece - 1 >= document_start(ends, query_piece * piece)
    )


def chip_pairs(blocks):
    return [(small, large) for large in range(1, blocks // 2) for small in range(large + 1)]


def plan_kernel(
    blocks,
    doc_hbm,
    table_hbm,
    k_hbm,
    v_hbm,
    q_hbm,
    g_hbm,
    plan_ref,
    flip0_ref,
    flip1_ref,
    index_ref,
    fetch_ref,
    middle_ref,
    k_ref,
    v_ref,
    rows_ref,
    *refs,
):
    *ahead_refs, doc_ref, table_ref, sem = refs
    pairs = [(doc_hbm, doc_ref), (table_hbm, table_ref), (k_hbm, k_ref), (v_hbm, v_ref)]
    width = k_ref.shape[1]
    for number, ahead_ref in enumerate(ahead_refs):
        head = number // 2
        pairs.append(((q_hbm, g_hbm)[number % 2].at[:, head * width : (head + 1) * width], ahead_ref))
    copies = [pltpu.make_async_copy(*pair, sem.at[number]) for number, pair in enumerate(pairs)]
    for copy in copies:
        copy.start()
    piece = k_ref.shape[0] // 2
    block = lax.axis_index("ctx")
    side = lax.axis_index("head")
    for copy in copies[:2]:
        copy.wait()
    ends = []
    running = 0
    for doc in range(doc_ref.shape[0] - 1):
        running = running + doc_ref[doc]
        ends.append(running)
    first, second = table_ref[0, 0], table_ref[1, 0]
    flips = jnp.minimum(first, second), jnp.maximum(first, second)

    half_way = blocks * piece
    start, stop = jnp.int32(0), jnp.int32(2 * half_way)
    for end in reversed(ends):
        start = jnp.where(end <= half_way, jnp.maximum(start, end), start)
        stop = jnp.where(end > half_way, end, stop)
    first_key = lax.div(start, piece)
    first_query = 2 * blocks - 1 - lax.div(stop - 1, piece)
    middle = jnp.int32(0)
    for other in range(blocks):
        for flip in flips:
            middle = middle | ((other >= first_query) & ((other ^ flip) >= first_key)).astype(jnp.int32)

    for place, number in enumerate((*ends, *flips, middle)):
        plan_ref[place] = number
    small, large = (lax.shift_right_logical(flip, 1) for flip in flips)
    flip0_ref[0] = small
    flip1_ref[0] = large
    pair = lax.shift_right_logical(large * (large + 1), 1) + small - 1
    index_ref[0] = pair
    fetch_ref[0] = pair + middle * len(chip_pairs(blocks))
    middle_ref[0] = middle
    for number, flip in enumerate(flips):
        odd = flip & 1
        source = block ^ odd
        upper = (source > (source ^ flip)).astype(jnp.int32) * (1 - middle * side)
        for place, value in ((2 * number, odd), (2 * number + 1, upper)):
            rows_ref[place : place + 1, :] = jnp.full((1, rows_ref.shape[1]), value.astype(F32))
    for copy in copies[2:]:
        copy.wait()


def make_plan(blocks, doc_lengths, table, keys, values, queries, out_grad):
    smem = pl.BlockSpec(memory_space=pltpu.SMEM)
    vmem = pl.BlockSpec(memory_space=pltpu.VMEM)
    hbm = pl.BlockSpec(memory_space=pltpu.HBM)
    scalar = jax.ShapeDtypeStruct((1,), jnp.int32)
    pair = jax.ShapeDtypeStruct(keys.shape, keys.dtype)
    return pl.pallas_call(
        lambda *refs: plan_kernel(blocks, *refs),
        out_shape=[jax.ShapeDtypeStruct((8,), jnp.int32)]
        + [scalar] * 5
        + [pair, pair, jax.ShapeDtypeStruct((8, keys.shape[1]), F32)]
        + [pair] * (2 * AHEAD),
        in_specs=[hbm] * 6,
        out_specs=[smem] * 6 + [vmem] * (3 + 2 * AHEAD),
        scratch_shapes=[
            pltpu.SMEM(doc_lengths.shape, jnp.int32),
            pltpu.SMEM(table.shape, jnp.int32),
            pltpu.SemaphoreType.DMA((4 + 2 * AHEAD,)),
        ],
        compiler_params=pltpu.CompilerParams(vmem_limit_bytes=SMALL),
        cost_estimate=pl.CostEstimate(flops=0, bytes_accessed=4 * keys.size, transcendentals=0),
        name="plan",
    )(
        *[
            pltpu.with_memory_space_constraint(part, pltpu.HBM)
            for part in (doc_lengths, table, keys, values, queries, out_grad)
        ]
    )


def message_kernel(rows_ref, k_ref, v_ref, k2_ref, v2_ref, *message_refs):
    piece = k_ref.shape[0] // 2
    halves = slice(0, piece), slice(piece, 2 * piece)
    for number, message_ref in enumerate(message_refs):
        odd = rows_ref[2 * number : 2 * number + 1, :] > 0.5
        upper = rows_ref[2 * number + 1 : 2 * number + 2, :] > 0.5
        for target, own_ref, sibling_ref in ((halves[0], k_ref, k2_ref), (halves[1], v_ref, v2_ref)):
            low, high = (
                jnp.where(odd, sibling_ref[half].astype(F32), own_ref[half].astype(F32)) for half in halves
            )
            message_ref[target] = jnp.where(upper, high, low).astype(message_ref.dtype)


def make_messages(rows, *pairs):
    vmem = pl.BlockSpec(memory_space=pltpu.VMEM)
    message = jax.ShapeDtypeStruct(pairs[0].shape, pairs[0].dtype)
    return pl.pallas_call(
        message_kernel,
        out_shape=[message] * 2,
        in_specs=[vmem] * 5,
        out_specs=[vmem] * 2,
        compiler_params=pltpu.CompilerParams(vmem_limit_bytes=SMALL),
        name="messages",
    )(rows, *pairs)


def sum_pairs_kernel(keep_ref, received_ref, *out_refs):
    rows = out_refs[0].shape[0]
    for place, out_ref in enumerate(out_refs):
        part = slice(place * rows, (place + 1) * rows)
        out_ref[...] = (keep_ref[part] + received_ref[part].astype(F32)).astype(out_ref.dtype)


def sum_own_kernel(rows_ref, own_ref, own_received_ref, *refs):
    *back_refs, total_ref = refs
    total = own_ref[...] + own_received_ref[...].astype(F32)
    for number, back_ref in enumerate(back_refs):
        odd = rows_ref[2 * number : 2 * number + 1, :] > 0.5
        total = total + jnp.where(odd, 0.0, back_ref[...].astype(F32))
    total_ref[...] = total


def sum_all_kernel(rows_ref, total_ref, *refs):
    *sibling_refs, key_ref, value_ref = refs
    piece = key_ref.shape[0]
    for out_ref, rows in ((key_ref, slice(0, piece)), (value_ref, slice(piece, 2 * piece))):
        total = total_ref[rows]
        for number, sibling_ref in enumerate(sibling_refs):
            odd = rows_ref[2 * number : 2 * number + 1, :] > 0.5
            total = total + jnp.where(odd, sibling_ref[rows].astype(F32), 0.0)
        out_ref[...] = total


def head_copies(heads, width, hbm_ref, vmem_ref, sem, out=False, first=0):
    copies = []
    for head in range(first, heads):
        columns = hbm_ref.at[:, head * width : (head + 1) * width]
        ends = (vmem_ref.at[head], columns) if out else (columns, vmem_ref.at[head])
        copies.append(pltpu.make_async_copy(*ends, sem.at[head]))
    return copies


def piece_rows(slot, piece):
    return pl.ds(pl.multiple_of(slot * piece, piece), piece)


def partner_tiles(ends, flips, blocks, piece, block, tiles, first):
    count = jnp.int32(first)
    for round_index, flip in enumerate(flips):
        other = block ^ flip
        for query_slot, query_piece, key_slot, key_piece in (
            (0, block, 2 * round_index + 2, other),
            (1, 2 * blocks - 1 - block, 2 * round_index + 2, other),
            (1, 2 * blocks - 1 - block, 2 * round_index + 3, 2 * blocks - 1 - other),
        ):
            active = sees(ends, piece, query_piece, key_piece)

            @pl.when(active)
            def _():
                tiles[0, count] = jnp.int32(query_slot)
                tiles[1, count] = jnp.int32(key_slot)
                tiles[2, count] = query_piece * piece
                tiles[3, count] = key_piece * piece

            count = count + active.astype(jnp.int32)
    return count


def tile_gradients(heads, piece, e_ref, dp_ref, scale_ref, delta_ref, q_ref, g_ref, dk_acc, dv_acc, together=4):
    width = q_ref.shape[2]

    def run(index, query_slot, key_slot, hand_on):
        query_rows = piece_rows(query_slot, piece)
        key_rows = piece_rows(key_slot, piece)

        def elementwise(group):
            lows, ds = [], []
            for head in range(group * together, (group + 1) * together):
                row = slice(head, head + 1)
                probs = e_ref[index, head] * scale_ref[index, row, :]
                lows.append(probs.astype(BF16))
                ds.append((probs * (dp_ref[index, head] - delta_ref[query_slot, row, :])).astype(BF16))
            return jnp.concatenate(lows, axis=1), jnp.concatenate(ds, axis=1)

        def products(group, probs, dscores, dk, dv):
            members = slice(group * together, (group + 1) * together)
            dv = dv + nn_dot(probs, g_ref[members, query_rows, :].reshape(together * piece, width))
            dk = dk + nn_dot(dscores, q_ref[members, query_rows, :].reshape(together * piece, width))
            hand_on(slice(group * together * piece, (group + 1) * together * piece), dscores)
            return dk, dv

        dk = jnp.zeros((piece, width), F32)
        dv = jnp.zeros((piece, width), F32)
        held = elementwise(0)
        for group in range(1, heads // together):
            following = elementwise(group)
            dk, dv = products(group - 1, *held, dk, dv)
            held = following
        dk, dv = products(heads // together - 1, *held, dk, dv)
        dk_acc[key_rows, :] += dk
        dv_acc[key_rows, :] += dv

    return run


def partner_kernel(
    blocks,
    heads,
    plan_hbm,
    q_hbm,
    g_hbm,
    k_ref,
    v_ref,
    first0_hbm,
    second0_hbm,
    first1_hbm,
    second1_hbm,
    *refs,
):
    ahead_refs, refs = refs[: 2 * AHEAD], refs[2 * AHEAD :]
    keep_ref, cross_ref, e_buf, dp_buf, ds_all, stat_l, delta_buf, q_ref, g_ref, kall, *refs = refs
    plan_ref, plan_sem, head_sem, pair_sem, vall, bias_buf, stat_m, stat_d, dk_acc, dv_acc, tiles = refs
    rows, width = k_ref.shape
    piece = rows // 2
    factor = width**-0.5
    block = lax.axis_index("ctx")
    side = lax.axis_index("head")
    rounds = 2
    own_tiles = 3
    slots = stat_m.shape[0]

    plan_copy = pltpu.make_async_copy(plan_hbm, plan_ref, plan_sem.at[0])
    plan_copy.start()
    arrivals_by_head = dict(
        enumerate(
            zip(
                head_copies(heads, width, q_hbm, q_ref, head_sem.at[0], first=AHEAD),
                head_copies(heads, width, g_hbm, g_ref, head_sem.at[1], first=AHEAD),
            ),
            start=AHEAD,
        )
    )
    for arrivals in arrivals_by_head.values():
        for arrival in arrivals:
            arrival.start()
    kall[:rows] = k_ref[...]
    vall[:rows] = v_ref[...]
    stat_m[...] = jnp.full_like(stat_m, 2 * MASKED)
    stat_l[...] = jnp.zeros_like(stat_l)
    stat_d[...] = jnp.zeros_like(stat_d)
    plan_copy.wait()
    docs = 3
    ends = [plan_ref[doc] for doc in range(docs)]
    flips = [plan_ref[docs], plan_ref[docs + 1]]
    middle = plan_ref[docs + 2]
    pairs = []
    for round_index, received in enumerate(((first0_hbm, second0_hbm), (first1_hbm, second1_hbm))):
        half = (block < (block ^ flips[round_index])).astype(jnp.int32) * (1 - middle * side)
        for both, where in zip(received, (half, 1 - half)):
            place = pl.ds(pl.multiple_of((2 * round_index + 2 + where) * piece, piece), piece)
            pairs += [(both.at[:piece], kall.at[place]), (both.at[piece:], vall.at[place])]
    pair_arrivals = [pltpu.make_async_copy(*pair, pair_sem.at[number]) for number, pair in enumerate(pairs)]
    for arrival in pair_arrivals:
        arrival.start()

    low_piece = block
    high_piece = 2 * blocks - 1 - block
    own = [(0, 0, low_piece, low_piece), (1, 1, high_piece, high_piece), (1, 0, high_piece, low_piece)]
    for index, (query_slot, key_slot, query_piece, key_piece) in enumerate(own):
        tiles[0, index] = jnp.int32(query_slot)
        tiles[1, index] = jnp.int32(key_slot)
        tiles[2, index] = query_piece * piece
        tiles[3, index] = key_piece * piece
    own_active = sees(ends, piece, high_piece, low_piece)
    count = partner_tiles(ends, flips, blocks, piece, block, tiles, own_tiles)

    def set_bias(index, slot):
        query_start = tiles[2, index]
        key_start = tiles[3, index]
        query_pos = query_start + lax.broadcasted_iota(jnp.int32, (1, piece), 1)
        starts = document_start(ends, query_pos)
        key_index = lax.broadcasted_iota(jnp.int32, (piece, piece), 0)
        seen = (key_index >= starts - key_start) & (key_index <= query_pos - key_start)
        bias_buf[slot] = jnp.where(seen, 0.0, MASKED)

    def head_scores(index, head, products, dprobs, query_slot, slot, from_diagonal):
        row = slice(head, head + 1)
        scores = products * (factor * LOG2E)
        if slot is not None:
            scores = scores + bias_buf[slot]
        if from_diagonal:
            top = stat_m[query_slot, row, :]
        else:
            top = jnp.max(scores, axis=0, keepdims=True)
        weights = jnp.exp2(scores - top)
        e_buf[index, head] = weights
        dp_buf[index, head] = dprobs
        stat_m[index, row, :] = top
        stat_l[index, row, :] = jnp.sum(weights, axis=0, keepdims=True)
        stat_d[index, row, :] = jnp.sum(weights * dprobs, axis=0, keepdims=True)

    def first_pass(from_diagonal, together=4):
        def make(index, slot):
            query_slot = tiles[0, index]
            query_rows = piece_rows(query_slot, piece)
            key_rows = piece_rows(tiles[1, index], piece)
            keys = kall[key_rows, :]
            values = vall[key_rows, :]
            for group in range(0, heads, together):
                members = slice(group, group + together)
                products = nt_dot(keys, q_ref[members, query_rows, :].reshape(together * piece, width))
                dprobs = nt_dot(values, g_ref[members, query_rows, :].reshape(together * piece, width))
                for member in range(together):
                    columns = slice(member * piece, (member + 1) * piece)
                    head_scores(
                        index, group + member, products[:, columns], dprobs[:, columns], query_slot, slot, from_diagonal
                    )

        def run(index, carry):
            whole = document_start(ends, tiles[2, index] + piece - 1) <= tiles[3, index]

            @pl.when(whole)
            def _():
                make(index, None)

            @pl.when(jnp.logical_not(whole))
            def _():
                set_bias(index, 0)
                make(index, 0)

            return carry

        return run

    for index in range(2):
        set_bias(index, index)
    for head in range(heads):
        if head < AHEAD:
            q_ref[head] = ahead_refs[2 * head][...]
            g_ref[head] = ahead_refs[2 * head + 1][...]
        else:
            for arrival in arrivals_by_head[head]:
                arrival.wait()
        for index in range(2):
            part = slice(index * piece, (index + 1) * piece)
            products = nt_dot(kall[part, :], q_ref[head, part, :])
            dprobs = nt_dot(vall[part, :], g_ref[head, part, :])
            head_scores(index, head, products, dprobs, index, index, False)
    dk_acc[...] = jnp.zeros_like(dk_acc)
    dv_acc[...] = jnp.zeros_like(dv_acc)
    for arrival in pair_arrivals:
        arrival.wait()
    begin = jnp.where(own_active, own_tiles - 1, own_tiles)
    lax.fori_loop(begin, count, first_pass(True), 0)
    redo = jnp.max(stat_l[...]) > 2.0**80
    lax.fori_loop(begin, jnp.where(redo, count, begin), first_pass(False), 0)

    lower = [tiles[0, slot] == 0 for slot in range(slots)]
    nothing = jnp.full((heads, piece), 2 * MASKED, F32)
    tops = [nothing, nothing]
    for slot in range(slots):
        top = stat_m[slot]
        tops[0] = jnp.maximum(tops[0], jnp.where(lower[slot], top, nothing))
        tops[1] = jnp.maximum(tops[1], jnp.where(lower[slot], nothing, top))
    scales = [jnp.exp2(stat_m[slot] - jnp.where(lower[slot], *tops)) for slot in range(slots)]
    zero = jnp.zeros((heads, piece), F32)
    totals, deltas = [zero, zero], [zero, zero]
    for slot in range(slots):
        part, share = scales[slot] * stat_l[slot], scales[slot] * stat_d[slot]
        totals = [totals[0] + jnp.where(lower[slot], part, zero), totals[1] + jnp.where(lower[slot], zero, part)]
        deltas = [deltas[0] + jnp.where(lower[slot], share, zero), deltas[1] + jnp.where(lower[slot], zero, share)]
    inverses = [1.0 / total for total in totals]
    for query_slot in range(2):
        delta_buf[query_slot] = deltas[query_slot] * inverses[query_slot]
    for slot in range(slots):
        stat_l[slot] = scales[slot] * jnp.where(lower[slot], *inverses)

    add_tile = tile_gradients(heads, piece, e_buf, dp_buf, stat_l, delta_buf, q_ref, g_ref, dk_acc, dv_acc)

    def second_pass(index, carry):
        def keep_dscores(columns, dscores):
            ds_all[index - own_tiles, :, columns] = dscores

        add_tile(index, tiles[0, index], tiles[1, index], keep_dscores)
        return carry

    lax.fori_loop(own_tiles, count, second_pass, 0)

    for place in range(rounds):
        base = place * rows
        for half, out_ref in ((side, keep_ref), (1 - side, cross_ref)):
            key_rows = pl.ds(pl.multiple_of((2 * place + 2 + half) * piece, piece), piece)
            out_ref[base : base + piece] = (dk_acc[key_rows, :] * factor).astype(out_ref.dtype)
            out_ref[base + piece : base + rows] = dv_acc[key_rows, :].astype(out_ref.dtype)


def own_kernel(
    blocks,
    heads,
    plan_ref,
    e_ref,
    dp_ref,
    ds_all,
    scale_ref,
    delta_ref,
    q_ref,
    g_ref,
    kall,
    dq_hbm,
    own_ref,
    own_cross_ref,
    dq_ref,
    out_sem,
    dk_acc,
    dv_acc,
    dqt_acc,
    tiles,
):
    _, rows, width = q_ref.shape
    piece = rows // 2
    factor = width**-0.5
    block = lax.axis_index("ctx")
    side = lax.axis_index("head")
    docs = 3
    own_tiles = 3
    ends = [plan_ref[doc] for doc in range(docs)]
    flips = [plan_ref[docs], plan_ref[docs + 1]]
    dk_acc[...] = jnp.zeros_like(dk_acc)
    dv_acc[...] = jnp.zeros_like(dv_acc)
    add_tile = tile_gradients(heads, piece, e_ref, dp_ref, scale_ref, delta_ref, q_ref, g_ref, dk_acc, dv_acc)

    def own_tile(query_slot, key_slot, index, first):
        keys_t = kall[piece_rows(key_slot, piece), :].T

        def add_query_gradient(columns, dscores):
            part = nn_dot(keys_t, dscores)
            if first:
                dqt_acc[query_slot, :, columns] = part
            else:
                dqt_acc[query_slot, :, columns] += part

        add_tile(index, query_slot, key_slot, add_query_gradient)

    def diagonal_tile(index, carry):
        own_tile(index, index, index, True)
        return carry

    lax.fori_loop(0, own_tiles - 1, diagonal_tile, 0)

    @pl.when(sees(ends, piece, 2 * blocks - 1 - block, block))
    def _():
        own_tile(1, 0, own_tiles - 1, False)

    def partner_tile(index, carry):
        keys_t = kall[piece_rows(tiles[1, index], piece), :].T
        dqt_acc[tiles[0, index]] += nn_dot(keys_t, ds_all[index])
        return carry

    lax.fori_loop(0, partner_tiles(ends, flips, blocks, piece, block, tiles, 0), partner_tile, 0)

    leaving = head_copies(heads, width, dq_hbm, dq_ref, out_sem, out=True)
    for head in range(heads):
        for query_slot in range(2):
            dq_ref[head, query_slot * piece : (query_slot + 1) * piece, :] = (
                (dqt_acc[query_slot, :, head * piece : (head + 1) * piece] * factor).astype(BF16).T
            )
        leaving[head].start()
    for half, out_ref in ((side, own_ref), (1 - side, own_cross_ref)):
        key_rows = pl.ds(pl.multiple_of(half * piece, piece), piece)
        out_ref[:piece] = (dk_acc[key_rows, :] * factor).astype(out_ref.dtype)
        out_ref[piece:] = dv_acc[key_rows, :].astype(out_ref.dtype)
    for copy in leaving:
        copy.wait()


def partner_attention(blocks, plan, queries, out_grad, keys, values, remote, ahead):
    rows, width = keys.shape
    heads = queries.shape[1] // width
    piece = rows // 2
    most = 7
    vmem = pl.BlockSpec(memory_space=pltpu.VMEM)
    hbm = pl.BlockSpec(memory_space=pltpu.HBM)
    anywhere = pl.BlockSpec(memory_space=pl.ANY)
    return pl.pallas_call(
        lambda *refs: partner_kernel(blocks, heads, *refs),
        out_shape=[
            jax.ShapeDtypeStruct((2 * rows, width), F32),
            jax.ShapeDtypeStruct((2 * rows, width), BF16),
            jax.ShapeDtypeStruct((most, heads, piece, piece), F32),
            jax.ShapeDtypeStruct((most, heads, piece, piece), F32),
            jax.ShapeDtypeStruct((most - 3, piece, heads * piece), BF16),
            jax.ShapeDtypeStruct((most, heads, piece), F32),
            jax.ShapeDtypeStruct((2, heads, piece), F32),
            jax.ShapeDtypeStruct((heads, rows, width), BF16),
            jax.ShapeDtypeStruct((heads, rows, width), BF16),
            jax.ShapeDtypeStruct((3 * rows, width), BF16),
        ],
        in_specs=[anywhere] + [hbm] * 2 + [vmem] * 2 + [anywhere] * 4 + [vmem] * (2 * AHEAD),
        out_specs=[vmem] * 10,
        scratch_shapes=[
            pltpu.SMEM(plan.shape, jnp.int32),
            pltpu.SemaphoreType.DMA((1,)),
            pltpu.SemaphoreType.DMA((2, heads)),
            pltpu.SemaphoreType.DMA((8,)),
            pltpu.VMEM((3 * rows, width), BF16),
            pltpu.VMEM((2, piece, piece), F32),
            pltpu.VMEM((most, heads, piece), F32),
            pltpu.VMEM((most, heads, piece), F32),
            pltpu.VMEM((3 * rows, width), F32),
            pltpu.VMEM((3 * rows, width), F32),
            pltpu.SMEM((4, most), jnp.int32),
        ],
        compiler_params=pltpu.CompilerParams(vmem_limit_bytes=VMEM_LIMITS[0]),
        cost_estimate=pl.CostEstimate(
            flops=7 * heads * 4 * 2 * piece * piece * width,
            bytes_accessed=4 * queries.size,
            transcendentals=7 * heads * piece * piece,
        ),
        name="partner_gradients",
    )(
        plan,
        *[pltpu.with_memory_space_constraint(part, pltpu.HBM) for part in (queries, out_grad)],
        keys,
        values,
        *remote,
        *ahead,
    )


def own_attention(blocks, plan, *held):
    heads, rows, width = held[-2].shape
    piece = rows // 2
    vmem = pl.BlockSpec(memory_space=pltpu.VMEM)
    smem = pl.BlockSpec(memory_space=pltpu.SMEM)
    hbm = pl.BlockSpec(memory_space=pltpu.HBM)
    return pl.pallas_call(
        lambda *refs: own_kernel(blocks, heads, *refs),
        out_shape=[
            jax.ShapeDtypeStruct((rows, heads * width), BF16),
            jax.ShapeDtypeStruct((rows, width), F32),
            jax.ShapeDtypeStruct((rows, width), BF16),
        ],
        in_specs=[smem] + [vmem] * 8,
        out_specs=[hbm, vmem, vmem],
        scratch_shapes=[
            pltpu.VMEM((heads, rows, width), BF16),
            pltpu.SemaphoreType.DMA((heads,)),
            pltpu.VMEM((rows, width), F32),
            pltpu.VMEM((rows, width), F32),
            pltpu.VMEM((2, width, heads * piece), F32),
            pltpu.SMEM((4, 4), jnp.int32),
        ],
        compiler_params=pltpu.CompilerParams(vmem_limit_bytes=VMEM_LIMITS[1]),
        cost_estimate=pl.CostEstimate(
            flops=3 * heads * 3 * 2 * piece * piece * width,
            bytes_accessed=6 * heads * rows * width,
            transcendentals=0,
        ),
        name="own_gradients",
    )(plan, *held)


def unwritten(like):
    return pl.pallas_call(
        lambda *refs: None,
        out_shape=[jax.ShapeDtypeStruct(like.shape, like.dtype)] * 2,
        out_specs=[pl.BlockSpec(memory_space=pl.ANY)] * 2,
        compiler_params=pltpu.CompilerParams(vmem_limit_bytes=SMALL),
        name="unwritten",
    )()


def swap(message):
    return lax.ppermute(message, "head", [(0, 1), (1, 0)])


def move(blocks, flip, message):
    return lax.ppermute(message, "ctx", [(block, block ^ 2 * flip) for block in range(blocks)]) if flip else message


def few_pairs(blocks):
    return len(chip_pairs(blocks)) <= 64


def one_by_one(blocks, flips, messages):
    branches = [partial(move, blocks, flip) for flip in range(blocks // 2)]
    return [lax.switch(flip.reshape(()), branches, message) for flip, message in zip(flips, messages)]


def fetch(blocks, index, flips, middle, messages):
    def without(pair, *messages):
        return (*[move(blocks, flip, message) for flip, message in zip(pair, messages)], *unwritten(messages[0]))

    def with_middle(pair, *messages):
        moved = [move(blocks, flip, message) for flip, message in zip(pair, messages)]
        return (*moved, *[swap(message) for message in moved])

    if few_pairs(blocks):
        branches = [partial(run, pair) for run in (without, with_middle) for pair in chip_pairs(blocks)]
        return lax.switch(index.reshape(()), branches, *messages)
    moved = one_by_one(blocks, flips, messages)
    swaps = [lambda a, b: tuple(unwritten(a)), lambda a, b: (swap(a), swap(b))]
    return (*moved, *lax.switch(middle.reshape(()), swaps, *moved))


def give_back(blocks, index, flips, messages, aside):
    def run(pair, first, second, aside):
        return move(blocks, pair[0], first), move(blocks, pair[1], second), swap(aside)

    if few_pairs(blocks):
        return lax.switch(index.reshape(()), [partial(run, pair) for pair in chip_pairs(blocks)], *messages, aside)
    return (*one_by_one(blocks, flips, messages), swap(aside))


def on_device(queries, key_vectors, value_vectors, out_grad, doc_lengths, partner_table):
    blocks = lax.axis_size("ctx")
    rows, width = key_vectors.shape

    def sibling(message):
        return lax.ppermute(message, "ctx", [(block, block ^ 1) for block in range(blocks)])

    plan, flip0, flip1, index, fetch_index, middle, keys, values, selectors, *ahead = make_plan(
        blocks, doc_lengths, partner_table, key_vectors, value_vectors, queries, out_grad
    )
    messages = make_messages(selectors, keys, values, sibling(key_vectors), sibling(value_vectors))
    first0, first1, second0, second1 = fetch(blocks, fetch_index, (flip0, flip1), middle, messages)
    keep, cross, *held = partner_attention(
        blocks, plan, queries, out_grad, keys, values, (first0, second0, first1, second1), ahead
    )
    received = swap(cross)
    query_grad, own, own_cross = own_attention(blocks, plan, *held)
    vmem = pl.BlockSpec(memory_space=pltpu.VMEM)
    message = jax.ShapeDtypeStruct((rows, width), BF16)
    sums = pl.pallas_call(
        sum_pairs_kernel,
        out_shape=[message] * 2,
        in_specs=[vmem] * 2,
        out_specs=[vmem] * 2,
        compiler_params=pltpu.CompilerParams(vmem_limit_bytes=SMALL),
        name="sum_over_heads",
    )(keep, received)
    *back, own_received = give_back(blocks, index, (flip0, flip1), sums, own_cross)
    traded = [sibling(part) for part in back]
    total = pl.pallas_call(
        sum_own_kernel,
        out_shape=jax.ShapeDtypeStruct((rows, width), F32),
        in_specs=[vmem] * 5,
        out_specs=vmem,
        compiler_params=pltpu.CompilerParams(vmem_limit_bytes=SMALL),
        cost_estimate=pl.CostEstimate(flops=4 * rows * width, bytes_accessed=14 * rows * width, transcendentals=0),
        name="sum_own",
    )(selectors, own, own_received, *back)
    grad = jax.ShapeDtypeStruct((rows // 2, width), F32)
    key_grad, value_grad = pl.pallas_call(
        sum_all_kernel,
        out_shape=[grad] * 2,
        in_specs=[vmem] * 4,
        out_specs=[vmem] * 2,
        compiler_params=pltpu.CompilerParams(vmem_limit_bytes=SMALL),
        name="sum_over_blocks",
    )(selectors, total, *traded)
    return query_grad, key_grad, value_grad


def solution(mesh):
    return jax.shard_map(
        on_device,
        mesh=mesh,
        in_specs=(P("ctx", "head"), P("ctx", None), P("ctx", None), P("ctx", "head"), P(), P()),
        out_specs=(P("ctx", "head"), P(("ctx", "head"), None), P(("ctx", "head"), None)),
        check_vma=False,
    )
```
